32 devices in a mesh: gx: 16 (over z, y, core), gy: 2 (over x).
Axes of the slice: x: 2, y: 2, z: 4, core: 2. Of those that a mesh axis runs over, the one named last changes fastest.
Arguments:
- species: float32 [48, 128, 32, 128], P(None, 'gx', 'gy'), may hold values from 0.2 to 2
- rate_matrices: float32 [128, 32, 2304], P('gx', 'gy'), may hold values from -20 to 10, as said below
- loss_rates: float32 [48], replicated, may hold values from 0.05 to 0.5
- sweeps: int32 [128, 32], P('gx', 'gy'), may hold values from 5 to 10, as said below
- flow_rows: float32 [128, 32, 128], P('gx', 'gy'), may hold values from -0.24 to 0.24
- flow_columns: float32 [128, 32, 128], P('gx', 'gy'), may hold values from -0.24 to 0.24
Outputs:
- transported: float32 [48, 128, 32, 128], P(None, 'gx', 'gy')
The draws below stay inside these ranges and needn't reach their ends.
Inputs may be any that keep to these rules, and one draw needn't show every extreme that they name: `rate_matrices`: each column's rate matrix times the time step, with a negative diagonal. Columns in rows 56 to 71 take 9 or 10 sweeps, all others 5 or 6; both 5 and 10 occur.
All inputs are finite; a program needn't handle non-finite values.
Results may differ from the reference program's by a relative error of at most 0.0003.
Values sent between devices are 32-bit elements; how exact they have to be, the bound alone decides.
A program may use at most 128 MiB of HBM per device.

```python
import math
import jax
import jax.numpy as jnp
from jax import lax

S = 48
NZ = 128
MAX_SWEEPS = 10
NX = 128
NY = 32


def draw_rate_matrices(key, part):
    first_key, second_key = jax.random.split(key)
    decay = jnp.exp(jax.random.uniform(first_key, (NX, NY, S), jnp.float32, jnp.log(2.0), jnp.log(20.0)))
    coupled = jnp.clip(jax.random.normal(second_key, (NX, NY, S, S), jnp.float32), -4.0, 4.0)
    radius = 0.8
    gamma_value = 1.0 + 0.5 ** 0.5
    spread = radius / S ** 0.5 * (1.0 / gamma_value + decay)[..., None]
    identity = jnp.eye(S, dtype=jnp.float32)
    matrices = identity * -decay[..., None] + (1.0 - identity) * spread * coupled
    return matrices.reshape(NX, NY, S * S)


def draw_sweeps(key, part):
    first_key, second_key = jax.random.split(key)
    light = jax.random.randint(first_key, (NX, NY), 5, 7, dtype=jnp.int32)
    heavy = jax.random.randint(second_key, (NX, NY), 9, 11, dtype=jnp.int32)
    row_index = jnp.arange(NX, dtype=jnp.int32)[:, None]
    inside = (row_index >= NX // 2 - NX // 16) & (row_index < NX // 2 + NX // 16)
    counts = jnp.where(inside, heavy, light)
    counts = counts.at[NX // 2, 0].set(10)
    return counts.at[0, 0].set(5)


def steps_of(stream_key, extent, cuts, smallest, high):
    def one(position, parts):
        draws = jax.random.uniform(jax.random.fold_in(jax.random.fold_in(stream_key, 6), position), (parts,), jnp.float32, smallest / len(cuts), high / len(cuts))
        return jnp.repeat(jnp.exp(draws), extent[position] // parts).reshape((-1,) + (1,) * (len(extent) - position - 1))

    loudness = one(*cuts[0])
    for cut in cuts[1:]:
        loudness = loudness * one(*cut)
    return loudness


def setup_inputs(seed: int = 0) -> dict:
    seeds = jax.random.split(jax.random.key(seed), 7)
    return {
        "species": jnp.clip(jnp.exp(math.log(2.0) - 2.3025851 * jax.random.uniform(seeds[0], (S, NX, NY, NZ), jnp.float32) ** steps_of(seeds[0], (S, NX, NY, NZ), ((1, 16), (2, 2)), -0.2, 0.2)), 0.2, 2.0),
        "rate_matrices": draw_rate_matrices(jax.random.fold_in(seeds[6], 71), 0),
        "loss_rates": jnp.clip(jnp.exp(jax.random.uniform(seeds[2], (S,), jnp.float32, math.log(0.05), math.log(0.5))), 0.05, 0.5),
        "sweeps": draw_sweeps(jax.random.fold_in(seeds[6], 71), 0),
        "flow_rows": jnp.clip(jax.random.uniform(seeds[4], (NX, NY, NZ), jnp.float32, -0.24, 0.24) * steps_of(seeds[4], (NX, NY, NZ), ((0, 16), (1, 2)), -0.4, 0.0), -0.24, 0.24),
        "flow_columns": jnp.clip(jax.random.uniform(seeds[5], (NX, NY, NZ), jnp.float32, -0.24, 0.24) * steps_of(seeds[5], (NX, NY, NZ), ((0, 16), (1, 2)), -0.4, 0.0), -0.24, 0.24),
    }


section_gamma = 1.0 + 0.5 ** 0.5


def linear_parts(matrices):
    species_count = matrices.shape[-1]
    identity = jnp.eye(species_count, dtype=jnp.float32)
    diagonal = jnp.sum(matrices * identity, axis=-1)
    coupling = section_gamma * (matrices * (1.0 - identity))
    scaled = 1.0 - section_gamma * diagonal
    return coupling, scaled


def product(matrices, values):
    return jnp.einsum('bij,bjn->bin', matrices, values, precision=lax.Precision.HIGHEST)


def tendency(matrices, values, loss_rates):
    return product(matrices, values) - loss_rates[:, None] * values * values


def advect(concentration, flow_first, flow_second):
    row_flux = jnp.maximum(flow_first[:-1], 0.0) * concentration[:, :-1] + jnp.minimum(flow_first[:-1], 0.0) * concentration[:, 1:]
    column_flux = jnp.maximum(flow_second[:, :-1], 0.0) * concentration[:, :, :-1] + jnp.minimum(flow_second[:, :-1], 0.0) * concentration[:, :, 1:]
    interior = concentration[:, 1:-1, 1:-1]
    return interior - (row_flux[:, 1:, 1:-1] - row_flux[:, :-1, 1:-1]) - (column_flux[:, 1:-1, 1:] - column_flux[:, 1:-1, :-1])


def reference(species, rate_matrices, loss_rates, sweeps, flow_rows, flow_columns):
    columns_first = jnp.transpose(species, (1, 2, 0, 3))
    matrices_all = rate_matrices.reshape(NX, NY, S, S)

    def react_row(pieces):
        values, matrices, counts = pieces
        coupling, scaled = linear_parts(matrices)

        def run_sweeps(source):
            solved = jnp.zeros_like(source)
            for sweep_index in range(MAX_SWEEPS):
                update = (source + product(coupling, solved)) / scaled[:, :, None]
                solved = jnp.where((sweep_index < counts)[:, None, None], update, solved)
            return solved

        section_one = run_sweeps(tendency(matrices, values, loss_rates))
        shifted = values + section_one
        second = run_sweeps(tendency(matrices, shifted, loss_rates) - 2.0 * section_one)
        return values + 1.5 * section_one + 0.5 * second

    reacted = lax.map(react_row, (columns_first, matrices_all, sweeps))
    reacted = jnp.transpose(reacted, (2, 0, 1, 3))
    flow_first = jnp.pad(flow_rows, ((1, 1), (1, 1), (0, 0)))
    flow_second = jnp.pad(flow_columns, ((1, 1), (1, 1), (0, 0)))

    def transport_one(single):
        current = single[None]
        for substep in range(2):
            padded = jnp.pad(current, ((0, 0), (1, 1), (1, 1), (0, 0)))
            current = advect(padded, flow_first, flow_second)
        return current[0]

    return lax.map(transport_one, reacted)
```

```python
import jax
import jax.numpy as jnp
from jax import lax
from jax.experimental import pallas as pl
from jax.experimental.pallas import tpu as pltpu
from jax.sharding import PartitionSpec as P

section_gamma = 1.0 + 0.5**0.5


def halves(x):
    hi = x.astype(jnp.bfloat16)
    return hi, (x - hi.astype(jnp.float32)).astype(jnp.bfloat16)


def left(x):
    hi, lo = halves(x)
    return jnp.concatenate([hi, lo, hi], axis=1)


def right(x):
    hi, lo = halves(x)
    return jnp.concatenate([hi, hi, lo], axis=0)


def mm(a, b):
    return jnp.dot(a, b, preferred_element_type=jnp.float32)


def react(matrix, v, count, loss, eye):
    diagonal = jnp.sum(jnp.where(eye, matrix, 0.0), axis=1, keepdims=True)
    inverse = 1.0 / (1.0 - section_gamma * diagonal)
    m1 = jnp.where(eye, 0.0, matrix * (section_gamma * inverse))
    right_1 = right(m1)
    m2 = mm(left(m1), right_1)
    left_2 = left(m2)
    m3 = mm(left_2, right_1)
    m4 = mm(left_2, right(m2))
    left_4 = left(m4)
    m5 = mm(left_4, right_1)
    p4 = jnp.where(eye, 1.0, 0.0) + m1 + m2 + m3
    even = jnp.where(count % 2 == 0, 1.0, 0.0)
    short = p4 + m4 + even * m5
    full = p4 + mm(left_4, right(short))
    left_p = left(jnp.where(count > 8, full, short))
    left_a = left(matrix)
    r1 = mm(left_a, right(v)) - loss * v * v
    k1 = mm(left_p, right(r1 * inverse))
    w = v + k1
    r2 = mm(left_a, right(w)) - loss * w * w - 2.0 * k1
    k2 = mm(left_p, right(r2 * inverse))
    return v + 1.5 * k1 + 0.5 * k2


def reaction_kernel(species_ref, rates_ref, loss_ref, sweeps_ref, out_ref, rows_ref):
    count, nx, ny, depth = species_ref.shape
    flat = species_ref.reshape(count * nx * ny, depth)
    eye = lax.broadcasted_iota(jnp.int32, (count, count), 0) == lax.broadcasted_iota(
        jnp.int32, (count, count), 1
    )
    loss = jnp.sum(jnp.where(eye, loss_ref[...], 0.0), axis=1, keepdims=True)
    halves_of_row = ny // 8

    @pl.loop(0, nx * halves_of_row)
    def _(octet):
        x = octet // halves_of_row
        first = pl.multiple_of((octet % halves_of_row) * 8, 8)
        for i in range(count):
            rows_ref[i * 8 : i * 8 + 8, 0:count] = rates_ref[
                x, pl.ds(first, 8), i * count : (i + 1) * count
            ]
        for j in range(8):
            y = first + j
            matrix = rows_ref[pl.ds(j, count, stride=8), :][:, :count]
            v = flat[pl.ds(x * ny + y, count, stride=nx * ny), :]
            out_ref[x, y] = react(matrix, v, sweeps_ref[x, y], loss, eye)


def reaction(species, rates, loss, sweeps):
    count, nx, ny, depth = species.shape
    vmem = pl.BlockSpec(memory_space=pltpu.VMEM)
    return pl.pallas_call(
        reaction_kernel,
        out_shape=jax.ShapeDtypeStruct((nx, ny, count, depth), jnp.float32),
        in_specs=[vmem, vmem, vmem, pl.BlockSpec(memory_space=pltpu.SMEM)],
        out_specs=vmem,
        scratch_shapes=[pltpu.VMEM((count * 8, 128), jnp.float32)],
        compiler_params=pltpu.CompilerParams(vmem_limit_bytes=40 * 2**20),
        name="reaction",
    )(species, rates, loss.reshape(1, count), sweeps)


def from_behind(array, axis, by):
    length = lax.axis_size(axis)
    pairs = [(i, i + by) for i in range(length) if 0 <= i + by < length]
    return lax.ppermute(array, axis, pairs)


def padded_2(array, sides, width):
    for axis, dim in sides:
        size, length = (lax.axis_size(axis), array.shape[dim])
        up = [(i, (i + 1) % size) for i in range(size - 1)]
        down = [(j, i) for i, j in up]
        last = lax.slice_in_dim(array, length - width, length, axis=dim)
        first = lax.slice_in_dim(array, 0, width, axis=dim)
        before = lax.ppermute(last, axis, up)
        after = lax.ppermute(first, axis, down)
        array = jnp.concatenate([before, array, after], axis=dim)
    return array


def advect(concentration, flow_first, flow_second):
    row_flux = (
        jnp.maximum(flow_first[:-1], 0.0) * concentration[:, :-1]
        + jnp.minimum(flow_first[:-1], 0.0) * concentration[:, 1:]
    )
    column_flux = (
        jnp.maximum(flow_second[:, :-1], 0.0) * concentration[:, :, :-1]
        + jnp.minimum(flow_second[:, :-1], 0.0) * concentration[:, :, 1:]
    )
    interior = concentration[:, 1:-1, 1:-1]
    return (
        interior
        - (row_flux[:, 1:, 1:-1] - row_flux[:, :-1, 1:-1])
        - (column_flux[:, 1:-1, 1:] - column_flux[:, 1:-1, :-1])
    )


def on_device(species, rate_matrices, loss_rates, sweeps, flow_rows, flow_columns):
    reacted = reaction(species, rate_matrices, loss_rates, sweeps)
    concentration = jnp.transpose(reacted, (2, 0, 1, 3))
    below_rows = from_behind(flow_rows[-1:], "gx", 1)
    below_columns = from_behind(flow_columns[:, -1:], "gy", 1)
    empty_row = jnp.zeros_like(below_rows)
    empty_column = jnp.zeros_like(below_columns)
    first_wide = jnp.concatenate([below_rows, flow_rows, empty_row], 0)
    first_wide = jnp.pad(first_wide, ((0, 0), (1, 1), (0, 0)))
    second_wide = jnp.concatenate([below_columns, flow_columns, empty_column], 1)
    second_wide = jnp.pad(second_wide, ((1, 1), (0, 0), (0, 0)))
    transported = concentration
    for substep in range(2):
        padded = padded_2(transported, (("gx", 1), ("gy", 2)), 1)
        transported = advect(padded, first_wide, second_wide)
    return transported


def solution(mesh):
    placed = (
        P(None, "gx", "gy", None),
        P("gx", "gy", None),
        P(),
        P("gx", "gy"),
        P("gx", "gy", None),
        P("gx", "gy", None),
    )
    return jax.shard_map(
        on_device, mesh=mesh, in_specs=placed, out_specs=P(None, "gx", "gy", None), check_vma=False
    )
```

```python
import jax
import jax.numpy as jnp
from jax import lax
from jax.experimental import pallas as pl
from jax.experimental.pallas import tpu as pltpu
from jax.sharding import PartitionSpec as P

section_gamma = 1.0 + 0.5**0.5


def halves(x):
    hi = x.astype(jnp.bfloat16)
    return hi, (x - hi.astype(jnp.float32)).astype(jnp.bfloat16)


def left(x):
    hi, lo = halves(x)
    return jnp.concatenate([hi, lo, hi], axis=1)


def right(x):
    hi, lo = halves(x)
    return jnp.concatenate([hi, hi, lo], axis=0)


def mm(a, b):
    return jnp.dot(a, b, preferred_element_type=jnp.float32)


def react(matrices, states, counts, loss, eye):
    def each(f, *lists):
        return [f(*parts) for parts in zip(*lists)]

    def inverse_of(a):
        diagonal = jnp.sum(jnp.where(eye, a, 0.0), axis=1, keepdims=True)
        return 1.0 / (1.0 - section_gamma * diagonal)

    def solve(lefts, sources):
        return each(mm, lefts, each(lambda r, i: right(r * i), sources, inverse))

    left_a = each(left, matrices)
    inverse = each(inverse_of, matrices)
    m1 = each(lambda a, i: jnp.where(eye, 0.0, a * (section_gamma * i)), matrices, inverse)
    right_1 = each(right, m1)
    m2 = each(mm, each(left, m1), right_1)
    av = each(mm, left_a, each(right, states))
    left_2 = each(left, m2)
    m3 = each(mm, left_2, right_1)
    m4 = each(mm, left_2, each(right, m2))
    r1 = each(lambda p, v: p - loss * v * v, av, states)
    left_4 = each(left, m4)
    m5 = each(mm, left_4, right_1)
    unit = jnp.where(eye, 1.0, 0.0)
    p4 = each(lambda a, b, c: unit + a + b + c, m1, m2, m3)
    short = each(
        lambda p, a, b, n: p + a + jnp.where(n % 2 == 0, 1.0, 0.0) * b, p4, m4, m5, counts
    )
    rest = each(mm, left_4, each(right, short))
    left_p = each(
        lambda p, q, s, n: left(jnp.where(n > 8, p + q, s)), p4, rest, short, counts
    )
    k1 = solve(left_p, r1)
    w = each(lambda v, k: v + k, states, k1)
    aw = each(mm, left_a, each(right, w))
    r2 = each(lambda p, u, k: p - loss * u * u - 2.0 * k, aw, w, k1)
    k2 = solve(left_p, r2)
    return each(lambda v, a, b: v + 1.5 * a + 0.5 * b, states, k1, k2)


def reaction_kernel(species_ref, rates_ref, loss_ref, sweeps_ref, out_ref, rows_ref):
    count, nx, ny, depth = species_ref.shape
    flat = species_ref.reshape(count * nx * ny, depth)
    eye = lax.broadcasted_iota(jnp.int32, (count, count), 0) == lax.broadcasted_iota(
        jnp.int32, (count, count), 1
    )
    loss = jnp.sum(jnp.where(eye, loss_ref[...], 0.0), axis=1, keepdims=True)
    halves_of_row = ny // 8

    @pl.loop(0, nx * halves_of_row)
    def _(octet):
        x = octet // halves_of_row
        first = pl.multiple_of((octet % halves_of_row) * 8, 8)
        for i in range(count):
            rows_ref[i * 8 : i * 8 + 8, 0:count] = rates_ref[
                x, pl.ds(first, 8), i * count : (i + 1) * count
            ]
        matrices = [rows_ref[pl.ds(j, count, stride=8), :][:, :count] for j in range(8)]
        states = [flat[pl.ds(x * ny + first + j, count, stride=nx * ny), :] for j in range(8)]
        counts = [sweeps_ref[x, first + j] for j in range(8)]
        for j, result in enumerate(react(matrices, states, counts, loss, eye)):
            out_ref[x, first + j] = result


def reaction(species, rates, loss, sweeps):
    count, nx, ny, depth = species.shape
    vmem = pl.BlockSpec(memory_space=pltpu.VMEM)
    return pl.pallas_call(
        reaction_kernel,
        out_shape=jax.ShapeDtypeStruct((nx, ny, count, depth), jnp.float32),
        in_specs=[vmem, vmem, vmem, pl.BlockSpec(memory_space=pltpu.SMEM)],
        out_specs=vmem,
        scratch_shapes=[pltpu.VMEM((count * 8, 128), jnp.float32)],
        compiler_params=pltpu.CompilerParams(vmem_limit_bytes=40 * 2**20),
        name="reaction",
    )(species, rates, loss.reshape(1, count), sweeps)


def from_behind(array, axis, by):
    length = lax.axis_size(axis)
    pairs = [(i, i + by) for i in range(length) if 0 <= i + by < length]
    return lax.ppermute(array, axis, pairs)


def padded_2(array, sides, width):
    for axis, dim in sides:
        size, length = (lax.axis_size(axis), array.shape[dim])
        up = [(i, (i + 1) % size) for i in range(size - 1)]
        down = [(j, i) for i, j in up]
        last = lax.slice_in_dim(array, length - width, length, axis=dim)
        first = lax.slice_in_dim(array, 0, width, axis=dim)
        before = lax.ppermute(last, axis, up)
        after = lax.ppermute(first, axis, down)
        array = jnp.concatenate([before, array, after], axis=dim)
    return array


def advect(concentration, flow_first, flow_second):
    row_flux = (
        jnp.maximum(flow_first[:-1], 0.0) * concentration[:, :-1]
        + jnp.minimum(flow_first[:-1], 0.0) * concentration[:, 1:]
    )
    column_flux = (
        jnp.maximum(flow_second[:, :-1], 0.0) * concentration[:, :, :-1]
        + jnp.minimum(flow_second[:, :-1], 0.0) * concentration[:, :, 1:]
    )
    interior = concentration[:, 1:-1, 1:-1]
    return (
        interior
        - (row_flux[:, 1:, 1:-1] - row_flux[:, :-1, 1:-1])
        - (column_flux[:, 1:-1, 1:] - column_flux[:, 1:-1, :-1])
    )


def on_device(species, rate_matrices, loss_rates, sweeps, flow_rows, flow_columns):
    reacted = reaction(species, rate_matrices, loss_rates, sweeps)
    concentration = jnp.transpose(reacted, (2, 0, 1, 3))
    below_rows = from_behind(flow_rows[-1:], "gx", 1)
    below_columns = from_behind(flow_columns[:, -1:], "gy", 1)
    empty_row = jnp.zeros_like(below_rows)
    empty_column = jnp.zeros_like(below_columns)
    first_wide = jnp.concatenate([below_rows, flow_rows, empty_row], 0)
    first_wide = jnp.pad(first_wide, ((0, 0), (1, 1), (0, 0)))
    second_wide = jnp.concatenate([below_columns, flow_columns, empty_column], 1)
    second_wide = jnp.pad(second_wide, ((1, 1), (0, 0), (0, 0)))
    transported = concentration
    for substep in range(2):
        padded = padded_2(transported, (("gx", 1), ("gy", 2)), 1)
        transported = advect(padded, first_wide, second_wide)
    return transported


def solution(mesh):
    placed = (
        P(None, "gx", "gy", None),
        P("gx", "gy", None),
        P(),
        P("gx", "gy"),
        P("gx", "gy", None),
        P("gx", "gy", None),
    )
    return jax.shard_map(
        on_device, mesh=mesh, in_specs=placed, out_specs=P(None, "gx", "gy", None), check_vma=False
    )
```

```python
import functools

import jax
import jax.numpy as jnp
from jax import lax
from jax.experimental import pallas as pl
from jax.experimental.pallas import tpu as pltpu
from jax.sharding import PartitionSpec as P

section_gamma = 1.0 + 0.5**0.5


def halves(x):
    hi = x.astype(jnp.bfloat16)
    return hi, (x - hi.astype(jnp.float32)).astype(jnp.bfloat16)


def left(x):
    hi, lo = halves(x)
    return jnp.concatenate([hi, lo, hi], axis=1)


def right(x):
    hi, lo = halves(x)
    return jnp.concatenate([hi, hi, lo], axis=0)


def mm(a, b):
    return jnp.dot(a, b, preferred_element_type=jnp.float32)


def react(matrices, states, counts, loss, eye):
    def each(f, *lists):
        return [f(*parts) for parts in zip(*lists)]

    def inverse_of(a):
        diagonal = jnp.sum(jnp.where(eye, a, 0.0), axis=1, keepdims=True)
        return 1.0 / (1.0 - section_gamma * diagonal)

    def solve(lefts, sources):
        return each(mm, lefts, each(lambda r, i: right(r * i), sources, inverse))

    left_a = each(left, matrices)
    inverse = each(inverse_of, matrices)
    m1 = each(lambda a, i: jnp.where(eye, 0.0, a * (section_gamma * i)), matrices, inverse)
    right_1 = each(right, m1)
    m2 = each(mm, each(left, m1), right_1)
    av = each(mm, left_a, each(right, states))
    left_2 = each(left, m2)
    m3 = each(mm, left_2, right_1)
    m4 = each(mm, left_2, each(right, m2))
    r1 = each(lambda p, v: p - loss * v * v, av, states)
    left_4 = each(left, m4)
    m5 = each(mm, left_4, right_1)
    unit = jnp.where(eye, 1.0, 0.0)
    p4 = each(lambda a, b, c: unit + a + b + c, m1, m2, m3)
    short = each(
        lambda p, a, b, n: p + a + jnp.where(n % 2 == 0, 1.0, 0.0) * b, p4, m4, m5, counts
    )
    rest = each(mm, left_4, each(right, short))
    left_p = each(
        lambda p, q, s, n: left(jnp.where(n > 8, p + q, s)), p4, rest, short, counts
    )
    k1 = solve(left_p, r1)
    w = each(lambda v, k: v + k, states, k1)
    aw = each(mm, left_a, each(right, w))
    r2 = each(lambda p, u, k: p - loss * u * u - 2.0 * k, aw, w, k1)
    k2 = solve(left_p, r2)
    return each(lambda v, a, b: v + 1.5 * a + 0.5 * b, states, k1, k2)


ways = tuple((dx, dy) for dx in (-1, 0, 1) for dy in (-1, 0, 1) if (dx, dy) != (0, 0))


def span(way, size, corner):
    if way == 0:
        return slice(2, 2 + size), slice(2, 2 + size)
    width = 1 if corner else 2
    if way < 0:
        return slice(2, 2 + width), slice(2 + size, 2 + size + width)
    return slice(2 + size - width, 2 + size), slice(2 - width, 2)


def slab_kernel(
    extent,
    species_ref,
    rates_ref,
    loss_ref,
    sweeps_ref,
    flow_rows_ref,
    flow_columns_ref,
    out_ref,
    cells,
    moved,
    flows,
    rates,
    flow_send,
    flow_recv,
    cell_send,
    cell_recv,
):
    count, nx, ny, depth = species_ref.shape
    here = (lax.axis_index("gx"), lax.axis_index("gy"))

    def there(way):
        found = None
        for part, position, size in zip(way, here, extent):
            if part:
                inside = position > 0 if part < 0 else position < size - 1
                found = inside if found is None else found & inside
        return found

    def halo(buffer, send, recv, index):
        way = ways[index]
        corner = way[0] != 0 and way[1] != 0
        rows, rows_to = span(way[0], nx, corner)
        columns, columns_to = span(way[1], ny, corner)
        return pltpu.make_async_remote_copy(
            src_ref=buffer.at[rows, columns],
            dst_ref=buffer.at[rows_to, columns_to],
            send_sem=send.at[index],
            recv_sem=recv.at[index],
            device_id=(here[0] + way[0], here[1] + way[1]),
            device_id_type=pl.DeviceIdType.MESH,
        )

    def start(buffer, send, recv, chosen):
        for index, way in enumerate(ways):
            if chosen(way):

                @pl.when(there(way))
                def _():
                    halo(buffer, send, recv, index).start()

    def finish(buffer, send, recv):
        for index, way in enumerate(ways):

            @pl.when(there(way))
            def _():
                halo(buffer, send, recv, index).wait_send()

            @pl.when(there((-way[0], -way[1])))
            def _():
                halo(buffer, send, recv, index).wait_recv()

    empty = jnp.zeros((ny + 4, count, depth), jnp.float32)
    for x in (0, 1, nx + 2, nx + 3):
        cells[x] = empty
    for y in (0, 1, ny + 2, ny + 3):
        cells[:, y] = jnp.zeros((nx + 4, count, depth), jnp.float32)
    flows[...] = jnp.zeros_like(flows)

    barrier = pltpu.get_barrier_semaphore()
    for way in ways:

        @pl.when(there(way))
        def _():
            pl.semaphore_signal(
                barrier,
                inc=1,
                device_id=(here[0] + way[0], here[1] + way[1]),
                device_id_type=pl.DeviceIdType.MESH,
            )

    beside = [
        1 + jnp.where(position > 0, 1, 0) + jnp.where(position < size - 1, 1, 0)
        for position, size in zip(here, extent)
    ]
    pl.semaphore_wait(barrier, beside[0] * beside[1] - 1)

    flow_lines = flows.reshape((nx + 4) * (ny + 4) * 8, depth)
    for x in range(nx):
        line = ((x + 2) * (ny + 4) + 2) * 8
        flow_lines[pl.ds(line, ny, stride=8), :] = flow_rows_ref[x]
        flow_lines[pl.ds(line + 1, ny, stride=8), :] = flow_columns_ref[x]
    start(flows, flow_send, flow_recv, lambda way: True)

    flat = species_ref.reshape(count * nx * ny, depth)
    octets = ny // 8
    eye = lax.broadcasted_iota(jnp.int32, (count, count), 0) == lax.broadcasted_iota(
        jnp.int32, (count, count), 1
    )
    loss = jnp.sum(jnp.where(eye, loss_ref[...], 0.0), axis=1, keepdims=True)

    @pl.loop(0, nx * octets)
    def _(octet):
        x = octet // octets
        first = pl.multiple_of((octet % octets) * 8, 8)
        base = pl.multiple_of(octet * (count * 8), 8)
        for i in range(count):
            rates[pl.ds(base + i * 8, 8), 0:count] = rates_ref[
                x, pl.ds(first, 8), i * count : (i + 1) * count
            ]

    def columns_of(groups, place):
        @pl.loop(0, groups)
        def _(group):
            places = [place(group * 8 + j) for j in range(8)]
            matrices = [
                rates[
                    pl.ds((x * octets + y // 8) * (count * 8) + y % 8, count, stride=8), :
                ][:, :count]
                for x, y in places
            ]
            states = [flat[pl.ds(x * ny + y, count, stride=nx * ny), :] for x, y in places]
            counts = [sweeps_ref[x, y] for x, y in places]
            for (x, y), result in zip(places, react(matrices, states, counts, loss, eye)):
                cells[x + 2, y + 2] = result

    inner = ny - 4
    columns_of(ny // 4, lambda i: (i // ny, i % ny))
    start(cells, cell_send, cell_recv, lambda way: way[0] < 0)
    columns_of(ny // 4, lambda i: (nx - 2 + i // ny, i % ny))
    start(cells, cell_send, cell_recv, lambda way: way[0] > 0)
    columns_of((nx - 4) // 2, lambda i: (2 + i // 4, i % 4 + i % 4 // 2 * inner))
    start(cells, cell_send, cell_recv, lambda way: way[0] == 0)
    columns_of((nx - 4) * inner // 8, lambda i: (2 + i // inner, 2 + i % inner))
    finish(flows, flow_send, flow_recv)
    finish(cells, cell_send, cell_recv)

    def substep(c, x, y):
        down = flows[x, y, 0:1, :]
        up = flows[x - 1, y, 0:1, :]
        after = flows[x, y, 1:2, :]
        before = flows[x, y - 1, 1:2, :]
        from_down = -jnp.minimum(down, 0.0)
        from_up = jnp.maximum(up, 0.0)
        from_after = -jnp.minimum(after, 0.0)
        from_before = jnp.maximum(before, 0.0)
        kept = (
            1.0
            - (jnp.maximum(down, 0.0) - jnp.minimum(up, 0.0))
            - (jnp.maximum(after, 0.0) - jnp.minimum(before, 0.0))
        )
        return (
            kept * c[x, y]
            + from_down * c[x + 1, y]
            + from_up * c[x - 1, y]
            + from_after * c[x, y + 1]
            + from_before * c[x, y - 1]
        )

    @pl.loop(1, nx + 3)
    def _(x):
        @pl.loop(0, (ny + 2) // 6)
        def _(part):
            for j in range(6):
                moved[x, part * 6 + j + 1] = substep(cells, x, part * 6 + j + 1)

    @pl.when(here[0] == extent[0] - 1)
    def _():
        moved[nx + 2] = empty

    @pl.when(here[1] == extent[1] - 1)
    def _():
        moved[:, ny + 2] = jnp.zeros((nx + 4, count, depth), jnp.float32)

    @pl.loop(0, nx)
    def _(x):
        @pl.loop(0, ny // 8)
        def _(part):
            for j in range(8):
                y = part * 8 + j
                out_ref[x, y] = substep(moved, x + 2, y + 2)


def on_device(extent, species, rate_matrices, loss_rates, sweeps, flow_rows, flow_columns):
    count, nx, ny, depth = species.shape
    vmem = pl.BlockSpec(memory_space=pltpu.VMEM)
    padded = pltpu.VMEM((nx + 4, ny + 4, count, depth), jnp.float32)
    transported = pl.pallas_call(
        functools.partial(slab_kernel, extent),
        out_shape=jax.ShapeDtypeStruct((nx, ny, count, depth), jnp.float32),
        in_specs=[vmem, vmem, vmem, pl.BlockSpec(memory_space=pltpu.SMEM), vmem, vmem],
        out_specs=vmem,
        scratch_shapes=[
            padded,
            padded,
            pltpu.VMEM((nx + 4, ny + 4, 8, depth), jnp.float32),
            pltpu.VMEM((nx * ny * count, 128), jnp.float32),
        ]
        + [pltpu.SemaphoreType.DMA((len(ways),))] * 4,
        compiler_params=pltpu.CompilerParams(
            collective_id=0, has_side_effects=True, vmem_limit_bytes=48 * 2**20
        ),
        name="slab",
    )(species, rate_matrices, loss_rates.reshape(1, count), sweeps, flow_rows, flow_columns)
    return jnp.transpose(transported, (2, 0, 1, 3))


def solution(mesh):
    placed = (
        P(None, "gx", "gy", None),
        P("gx", "gy", None),
        P(),
        P("gx", "gy"),
        P("gx", "gy", None),
        P("gx", "gy", None),
    )
    extent = (mesh.shape["gx"], mesh.shape["gy"])
    return jax.shard_map(
        functools.partial(on_device, extent), mesh=mesh, in_specs=placed, out_specs=P(None, "gx", "gy", None), check_vma=False
    )
```

```python
import functools

import jax
import jax.numpy as jnp
from jax import lax
from jax.experimental import pallas as pl
from jax.experimental.pallas import tpu as pltpu
from jax.sharding import PartitionSpec as P

section_gamma = 1.0 + 0.5**0.5


def halves(x):
    hi = x.astype(jnp.bfloat16)
    return hi, (x - hi.astype(jnp.float32)).astype(jnp.bfloat16)


def left(x):
    hi, lo = halves(x)
    return jnp.concatenate([hi, lo, hi], axis=1)


def right(x):
    hi, lo = halves(x)
    return jnp.concatenate([hi, hi, lo], axis=0)


def mm(a, b):
    return jnp.dot(a, b, preferred_element_type=jnp.float32)


def react(matrices, states, counts, loss, eye):
    def each(f, *lists):
        return [f(*parts) for parts in zip(*lists)]

    def inverse_of(a):
        diagonal = jnp.sum(jnp.where(eye, a, 0.0), axis=1, keepdims=True)
        return 1.0 / (1.0 - section_gamma * diagonal)

    def solve(lefts, sources):
        return each(mm, lefts, each(lambda r, i: right(r * i), sources, inverse))

    left_a = each(left, matrices)
    inverse = each(inverse_of, matrices)
    m1 = each(lambda a, i: jnp.where(eye, 0.0, a * (section_gamma * i)), matrices, inverse)
    right_1 = each(right, m1)
    m2 = each(mm, each(left, m1), right_1)
    av = each(mm, left_a, each(right, states))
    left_2 = each(left, m2)
    m3 = each(mm, left_2, right_1)
    m4 = each(mm, left_2, each(right, m2))
    r1 = each(lambda p, v: p - loss * v * v, av, states)
    left_4 = each(left, m4)
    m5 = each(mm, left_4, right_1)
    unit = jnp.where(eye, 1.0, 0.0)
    p4 = each(lambda a, b, c: unit + a + b + c, m1, m2, m3)
    short = each(
        lambda p, a, b, n: p + a + jnp.where(n % 2 == 0, 1.0, 0.0) * b, p4, m4, m5, counts
    )
    rest = each(mm, left_4, each(right, short))
    left_p = each(
        lambda p, q, s, n: left(jnp.where(n > 8, p + q, s)), p4, rest, short, counts
    )
    k1 = solve(left_p, r1)
    w = each(lambda v, k: v + k, states, k1)
    aw = each(mm, left_a, each(right, w))
    r2 = each(lambda p, u, k: p - loss * u * u - 2.0 * k, aw, w, k1)
    k2 = solve(left_p, r2)
    return each(lambda v, a, b: v + 1.5 * a + 0.5 * b, states, k1, k2)


ways = tuple((dx, dy) for dx in (-1, 0, 1) for dy in (-1, 0, 1) if (dx, dy) != (0, 0))


def span(way, size, corner):
    if way == 0:
        return slice(2, 2 + size), slice(2, 2 + size)
    width = 1 if corner else 2
    if way < 0:
        return slice(2, 2 + width), slice(2 + size, 2 + size + width)
    return slice(2 + size - width, 2 + size), slice(2 - width, 2)


def slab_kernel(
    extent,
    species_hbm,
    rates_hbm,
    loss_ref,
    sweeps_hbm,
    flow_rows_hbm,
    flow_columns_hbm,
    out_ref,
    species_ref,
    rates_ref,
    sweeps_ref,
    flow_rows_ref,
    flow_columns_ref,
    fetch,
    cells,
    moved,
    flows,
    rates,
    flow_send,
    flow_recv,
    cell_send,
    cell_recv,
):
    count, nx, ny, depth = species_ref.shape
    fetches = [
        pltpu.make_async_copy(source, target, fetch.at[k])
        for k, (source, target) in enumerate(
            [
                (flow_rows_hbm, flow_rows_ref),
                (flow_columns_hbm, flow_columns_ref),
                (rates_hbm, rates_ref),
                (sweeps_hbm, sweeps_ref),
                (species_hbm, species_ref),
            ]
        )
    ]
    for copy in fetches:
        copy.start()
    here = (lax.axis_index("gx"), lax.axis_index("gy"))

    def there(way):
        found = None
        for part, position, size in zip(way, here, extent):
            if part:
                inside = position > 0 if part < 0 else position < size - 1
                found = inside if found is None else found & inside
        return found

    def halo(buffer, send, recv, index):
        way = ways[index]
        corner = way[0] != 0 and way[1] != 0
        rows, rows_to = span(way[0], nx, corner)
        columns, columns_to = span(way[1], ny, corner)
        return pltpu.make_async_remote_copy(
            src_ref=buffer.at[rows, columns],
            dst_ref=buffer.at[rows_to, columns_to],
            send_sem=send.at[index],
            recv_sem=recv.at[index],
            device_id=(here[0] + way[0], here[1] + way[1]),
            device_id_type=pl.DeviceIdType.MESH,
        )

    def start(buffer, send, recv, chosen):
        for index, way in enumerate(ways):
            if chosen(way):

                @pl.when(there(way))
                def _():
                    halo(buffer, send, recv, index).start()

    def finish(buffer, send, recv):
        for index, way in enumerate(ways):

            @pl.when(there(way))
            def _():
                halo(buffer, send, recv, index).wait_send()

            @pl.when(there((-way[0], -way[1])))
            def _():
                halo(buffer, send, recv, index).wait_recv()

    empty = jnp.zeros((ny + 4, count, depth), jnp.float32)
    for x in (0, 1, nx + 2, nx + 3):
        cells[x] = empty
    for y in (0, 1, ny + 2, ny + 3):
        cells[:, y] = jnp.zeros((nx + 4, count, depth), jnp.float32)
    flows[...] = jnp.zeros_like(flows)

    barrier = pltpu.get_barrier_semaphore()
    for way in ways:

        @pl.when(there(way))
        def _():
            pl.semaphore_signal(
                barrier,
                inc=1,
                device_id=(here[0] + way[0], here[1] + way[1]),
                device_id_type=pl.DeviceIdType.MESH,
            )

    beside = [
        1 + jnp.where(position > 0, 1, 0) + jnp.where(position < size - 1, 1, 0)
        for position, size in zip(here, extent)
    ]
    pl.semaphore_wait(barrier, beside[0] * beside[1] - 1)

    fetches[0].wait()
    fetches[1].wait()
    flow_lines = flows.reshape((nx + 4) * (ny + 4) * 8, depth)
    for x in range(nx):
        line = ((x + 2) * (ny + 4) + 2) * 8
        flow_lines[pl.ds(line, ny, stride=8), :] = flow_rows_ref[x]
        flow_lines[pl.ds(line + 1, ny, stride=8), :] = flow_columns_ref[x]
    start(flows, flow_send, flow_recv, lambda way: True)

    flat = species_ref.reshape(count * nx * ny, depth)
    octets = ny // 8
    eye = lax.broadcasted_iota(jnp.int32, (count, count), 0) == lax.broadcasted_iota(
        jnp.int32, (count, count), 1
    )
    loss = jnp.sum(jnp.where(eye, loss_ref[...], 0.0), axis=1, keepdims=True)

    fetches[2].wait()

    @pl.loop(0, nx * octets)
    def _(octet):
        x = octet // octets
        first = pl.multiple_of((octet % octets) * 8, 8)
        base = pl.multiple_of(octet * (count * 8), 8)
        for i in range(count):
            rates[pl.ds(base + i * 8, 8), 0:count] = rates_ref[
                x, pl.ds(first, 8), i * count : (i + 1) * count
            ]

    def columns_of(groups, place):
        @pl.loop(0, groups)
        def _(group):
            places = [place(group * 16 + j) for j in range(16)]
            matrices = [
                rates[
                    pl.ds((x * octets + y // 8) * (count * 8) + y % 8, count, stride=8), :
                ][:, :count]
                for x, y in places
            ]
            states = [flat[pl.ds(x * ny + y, count, stride=nx * ny), :] for x, y in places]
            counts = [sweeps_ref[x, y] for x, y in places]
            for (x, y), result in zip(places, react(matrices, states, counts, loss, eye)):
                cells[x + 2, y + 2] = result

    fetches[3].wait()
    fetches[4].wait()
    inner = ny - 4
    columns_of(ny // 8, lambda i: (i // ny, i % ny))
    start(cells, cell_send, cell_recv, lambda way: way[0] < 0)
    columns_of(ny // 8, lambda i: (nx - 2 + i // ny, i % ny))
    start(cells, cell_send, cell_recv, lambda way: way[0] > 0)
    columns_of((nx - 4) // 4, lambda i: (2 + i // 4, i % 4 + i % 4 // 2 * inner))
    start(cells, cell_send, cell_recv, lambda way: way[0] == 0)
    columns_of((nx - 4) * inner // 16, lambda i: (2 + i // inner, 2 + i % inner))
    finish(flows, flow_send, flow_recv)
    finish(cells, cell_send, cell_recv)

    def substep(c, x, y):
        down = flows[x, y, 0:1, :]
        up = flows[x - 1, y, 0:1, :]
        after = flows[x, y, 1:2, :]
        before = flows[x, y - 1, 1:2, :]
        from_down = -jnp.minimum(down, 0.0)
        from_up = jnp.maximum(up, 0.0)
        from_after = -jnp.minimum(after, 0.0)
        from_before = jnp.maximum(before, 0.0)
        kept = (
            1.0
            - (jnp.maximum(down, 0.0) - jnp.minimum(up, 0.0))
            - (jnp.maximum(after, 0.0) - jnp.minimum(before, 0.0))
        )
        return (
            kept * c[x, y]
            + from_down * c[x + 1, y]
            + from_up * c[x - 1, y]
            + from_after * c[x, y + 1]
            + from_before * c[x, y - 1]
        )

    @pl.loop(1, nx + 3)
    def _(x):
        @pl.loop(0, (ny + 2) // 6)
        def _(part):
            for j in range(6):
                moved[x, part * 6 + j + 1] = substep(cells, x, part * 6 + j + 1)

    @pl.when(here[0] == extent[0] - 1)
    def _():
        moved[nx + 2] = empty

    @pl.when(here[1] == extent[1] - 1)
    def _():
        moved[:, ny + 2] = jnp.zeros((nx + 4, count, depth), jnp.float32)

    @pl.loop(0, nx)
    def _(x):
        @pl.loop(0, ny // 8)
        def _(part):
            for j in range(8):
                y = part * 8 + j
                out_ref[x, y] = substep(moved, x + 2, y + 2)


def on_device(extent, species, rate_matrices, loss_rates, sweeps, flow_rows, flow_columns):
    count, nx, ny, depth = species.shape
    vmem = pl.BlockSpec(memory_space=pltpu.VMEM)
    hbm = pl.BlockSpec(memory_space=pltpu.HBM)
    padded = pltpu.VMEM((nx + 4, ny + 4, count, depth), jnp.float32)
    transported = pl.pallas_call(
        functools.partial(slab_kernel, extent),
        out_shape=jax.ShapeDtypeStruct((nx, ny, count, depth), jnp.float32),
        in_specs=[hbm, hbm, vmem, hbm, hbm, hbm],
        out_specs=vmem,
        scratch_shapes=[
            pltpu.VMEM(species.shape, jnp.float32),
            pltpu.VMEM(rate_matrices.shape, jnp.float32),
            pltpu.SMEM(sweeps.shape, jnp.int32),
            pltpu.VMEM(flow_rows.shape, jnp.float32),
            pltpu.VMEM(flow_columns.shape, jnp.float32),
            pltpu.SemaphoreType.DMA((5,)),
            padded,
            padded,
            pltpu.VMEM((nx + 4, ny + 4, 8, depth), jnp.float32),
            pltpu.VMEM((nx * ny * count, 128), jnp.float32),
        ]
        + [pltpu.SemaphoreType.DMA((len(ways),))] * 4,
        compiler_params=pltpu.CompilerParams(
            collective_id=0, has_side_effects=True, vmem_limit_bytes=60 * 2**20
        ),
        name="slab",
    )(species, rate_matrices, loss_rates.reshape(1, count), sweeps, flow_rows, flow_columns)
    return jnp.transpose(transported, (2, 0, 1, 3))


def solution(mesh):
    placed = (
        P(None, "gx", "gy", None),
        P("gx", "gy", None),
        P(),
        P("gx", "gy"),
        P("gx", "gy", None),
        P("gx", "gy", None),
    )
    extent = (mesh.shape["gx"], mesh.shape["gy"])
    return jax.shard_map(
        functools.partial(on_device, extent), mesh=mesh, in_specs=placed, out_specs=P(None, "gx", "gy", None), check_vma=False
    )
```

```python
import functools

import jax
import jax.numpy as jnp
from jax import lax
from jax.experimental import pallas as pl
from jax.experimental.pallas import tpu as pltpu
from jax.sharding import PartitionSpec as P

section_gamma = 1.0 + 0.5**0.5


def halves(x):
    hi = x.astype(jnp.bfloat16)
    return hi, (x - hi.astype(jnp.float32)).astype(jnp.bfloat16)


def left(x):
    hi, lo = halves(x)
    return jnp.concatenate([hi, lo, hi], axis=1)


def right(x):
    hi, lo = halves(x)
    return jnp.concatenate([hi, hi, lo], axis=0)


def mm(a, b):
    return jnp.dot(a, b, preferred_element_type=jnp.float32)


def react(matrices, states, counts, loss, eye):
    def each(f, *lists):
        return [f(*parts) for parts in zip(*lists)]

    def inverse_of(a):
        diagonal = jnp.sum(jnp.where(eye, a, 0.0), axis=1, keepdims=True)
        return 1.0 / (1.0 - section_gamma * diagonal)

    def solve(lefts, sources):
        return each(mm, lefts, each(lambda r, i: right(r * i), sources, inverse))

    left_a = each(left, matrices)
    inverse = each(inverse_of, matrices)
    m1 = each(lambda a, i: jnp.where(eye, 0.0, a * (section_gamma * i)), matrices, inverse)
    right_1 = each(right, m1)
    m2 = each(mm, each(left, m1), right_1)
    av = each(mm, left_a, each(right, states))
    left_2 = each(left, m2)
    m3 = each(mm, left_2, right_1)
    m4 = each(mm, left_2, each(right, m2))
    r1 = each(lambda p, v: p - loss * v * v, av, states)
    left_4 = each(left, m4)
    m5 = each(mm, left_4, right_1)
    unit = jnp.where(eye, 1.0, 0.0)
    p4 = each(lambda a, b, c: unit + a + b + c, m1, m2, m3)
    short = each(
        lambda p, a, b, n: p + a + jnp.where(n % 2 == 0, 1.0, 0.0) * b, p4, m4, m5, counts
    )
    rest = each(mm, left_4, each(right, short))
    left_p = each(
        lambda p, q, s, n: left(jnp.where(n > 8, p + q, s)), p4, rest, short, counts
    )
    k1 = solve(left_p, r1)
    w = each(lambda v, k: v + k, states, k1)
    aw = each(mm, left_a, each(right, w))
    r2 = each(lambda p, u, k: p - loss * u * u - 2.0 * k, aw, w, k1)
    k2 = solve(left_p, r2)
    return each(lambda v, a, b: v + 1.5 * a + 0.5 * b, states, k1, k2)


ways = tuple((dx, dy) for dx in (-1, 0, 1) for dy in (-1, 0, 1) if (dx, dy) != (0, 0))


def span(way, size, corner):
    if way == 0:
        return slice(2, 2 + size), slice(2, 2 + size)
    width = 1 if corner else 2
    if way < 0:
        return slice(2, 2 + width), slice(2 + size, 2 + size + width)
    return slice(2 + size - width, 2 + size), slice(2 - width, 2)


def slab_kernel(
    extent,
    species_hbm,
    rates_hbm,
    loss_ref,
    sweeps_hbm,
    flow_rows_hbm,
    flow_columns_hbm,
    out_ref,
    species_ref,
    rates_ref,
    sweeps_ref,
    flow_rows_ref,
    flow_columns_ref,
    fetch,
    cells,
    moved,
    flows,
    rates,
    flow_send,
    flow_recv,
    cell_send,
    cell_recv,
):
    count, nx, ny, depth = species_ref.shape
    fetches = [
        pltpu.make_async_copy(source, target, fetch.at[k])
        for k, (source, target) in enumerate(
            [
                (flow_rows_hbm, flow_rows_ref),
                (flow_columns_hbm, flow_columns_ref),
                (rates_hbm, rates_ref),
                (sweeps_hbm, sweeps_ref),
                (species_hbm, species_ref),
            ]
        )
    ]
    for copy in fetches:
        copy.start()
    here = (lax.axis_index("gx"), lax.axis_index("gy"))

    def there(way):
        found = None
        for part, position, size in zip(way, here, extent):
            if part:
                inside = position > 0 if part < 0 else position < size - 1
                found = inside if found is None else found & inside
        return found

    def halo(buffer, send, recv, index):
        way = ways[index]
        corner = way[0] != 0 and way[1] != 0
        rows, rows_to = span(way[0], nx, corner)
        columns, columns_to = span(way[1], ny, corner)
        return pltpu.make_async_remote_copy(
            src_ref=buffer.at[rows, columns],
            dst_ref=buffer.at[rows_to, columns_to],
            send_sem=send.at[index],
            recv_sem=recv.at[index],
            device_id=(here[0] + way[0], here[1] + way[1]),
            device_id_type=pl.DeviceIdType.MESH,
        )

    def start(buffer, send, recv, chosen):
        for index, way in enumerate(ways):
            if chosen(way):

                @pl.when(there(way))
                def _():
                    halo(buffer, send, recv, index).start()

    def finish(buffer, send, recv):
        for index, way in enumerate(ways):

            @pl.when(there(way))
            def _():
                halo(buffer, send, recv, index).wait_send()

            @pl.when(there((-way[0], -way[1])))
            def _():
                halo(buffer, send, recv, index).wait_recv()

    empty = jnp.zeros((ny + 4, count, depth), jnp.float32)
    for x in (0, 1, nx + 2, nx + 3):
        cells[x] = empty
    for y in (0, 1, ny + 2, ny + 3):
        cells[:, y] = jnp.zeros((nx + 4, count, depth), jnp.float32)
    flows[...] = jnp.zeros_like(flows)

    barrier = pltpu.get_barrier_semaphore()
    for way in ways:

        @pl.when(there(way))
        def _():
            pl.semaphore_signal(
                barrier,
                inc=1,
                device_id=(here[0] + way[0], here[1] + way[1]),
                device_id_type=pl.DeviceIdType.MESH,
            )

    beside = [
        1 + jnp.where(position > 0, 1, 0) + jnp.where(position < size - 1, 1, 0)
        for position, size in zip(here, extent)
    ]
    pl.semaphore_wait(barrier, beside[0] * beside[1] - 1)

    fetches[0].wait()
    fetches[1].wait()
    flow_lines = flows.reshape((nx + 4) * (ny + 4) * 8, depth)
    for x in range(nx):
        line = ((x + 2) * (ny + 4) + 2) * 8
        flow_lines[pl.ds(line, ny, stride=8), :] = flow_rows_ref[x]
        flow_lines[pl.ds(line + 1, ny, stride=8), :] = flow_columns_ref[x]
    start(flows, flow_send, flow_recv, lambda way: True)

    out_lines = out_ref.reshape(count * nx * ny, depth)
    flat = species_ref.reshape(count * nx * ny, depth)
    octets = ny // 8
    eye = lax.broadcasted_iota(jnp.int32, (count, count), 0) == lax.broadcasted_iota(
        jnp.int32, (count, count), 1
    )
    loss = jnp.sum(jnp.where(eye, loss_ref[...], 0.0), axis=1, keepdims=True)

    fetches[2].wait()

    @pl.loop(0, nx * octets)
    def _(octet):
        x = octet // octets
        first = pl.multiple_of((octet % octets) * 8, 8)
        base = pl.multiple_of(octet * (count * 8), 8)
        for i in range(count):
            rates[pl.ds(base + i * 8, 8), 0:count] = rates_ref[
                x, pl.ds(first, 8), i * count : (i + 1) * count
            ]

    def columns_of(groups, place):
        @pl.loop(0, groups)
        def _(group):
            places = [place(group * 16 + j) for j in range(16)]
            matrices = [
                rates[
                    pl.ds((x * octets + y // 8) * (count * 8) + y % 8, count, stride=8), :
                ][:, :count]
                for x, y in places
            ]
            states = [flat[pl.ds(x * ny + y, count, stride=nx * ny), :] for x, y in places]
            counts = [sweeps_ref[x, y] for x, y in places]
            for (x, y), result in zip(places, react(matrices, states, counts, loss, eye)):
                cells[x + 2, y + 2] = result

    fetches[3].wait()
    fetches[4].wait()
    inner = ny - 4
    columns_of(ny // 8, lambda i: (i // ny, i % ny))
    start(cells, cell_send, cell_recv, lambda way: way[0] < 0)
    columns_of(ny // 8, lambda i: (nx - 2 + i // ny, i % ny))
    start(cells, cell_send, cell_recv, lambda way: way[0] > 0)
    columns_of((nx - 4) // 4, lambda i: (2 + i // 4, i % 4 + i % 4 // 2 * inner))
    start(cells, cell_send, cell_recv, lambda way: way[0] == 0)
    columns_of((nx - 4) * inner // 16, lambda i: (2 + i // inner, 2 + i % inner))
    finish(flows, flow_send, flow_recv)
    finish(cells, cell_send, cell_recv)

    def substep(c, x, y):
        down = flows[x, y, 0:1, :]
        up = flows[x - 1, y, 0:1, :]
        after = flows[x, y, 1:2, :]
        before = flows[x, y - 1, 1:2, :]
        from_down = -jnp.minimum(down, 0.0)
        from_up = jnp.maximum(up, 0.0)
        from_after = -jnp.minimum(after, 0.0)
        from_before = jnp.maximum(before, 0.0)
        kept = (
            1.0
            - (jnp.maximum(down, 0.0) - jnp.minimum(up, 0.0))
            - (jnp.maximum(after, 0.0) - jnp.minimum(before, 0.0))
        )
        return (
            kept * c[x, y]
            + from_down * c[x + 1, y]
            + from_up * c[x - 1, y]
            + from_after * c[x, y + 1]
            + from_before * c[x, y - 1]
        )

    @pl.loop(1, nx + 3)
    def _(x):
        @pl.loop(0, (ny + 2) // 6)
        def _(part):
            for j in range(6):
                moved[x, part * 6 + j + 1] = substep(cells, x, part * 6 + j + 1)

    @pl.when(here[0] == extent[0] - 1)
    def _():
        moved[nx + 2] = empty

    @pl.when(here[1] == extent[1] - 1)
    def _():
        moved[:, ny + 2] = jnp.zeros((nx + 4, count, depth), jnp.float32)

    @pl.loop(0, nx)
    def _(x):
        @pl.loop(0, ny // 8)
        def _(part):
            for j in range(8):
                y = part * 8 + j
                out_lines[pl.ds(x * ny + y, count, stride=nx * ny), :] = substep(
                    moved, x + 2, y + 2
                )


def on_device(extent, species, rate_matrices, loss_rates, sweeps, flow_rows, flow_columns):
    count, nx, ny, depth = species.shape
    vmem = pl.BlockSpec(memory_space=pltpu.VMEM)
    hbm = pl.BlockSpec(memory_space=pltpu.HBM)
    padded = pltpu.VMEM((nx + 4, ny + 4, count, depth), jnp.float32)
    return pl.pallas_call(
        functools.partial(slab_kernel, extent),
        out_shape=jax.ShapeDtypeStruct(species.shape, jnp.float32),
        in_specs=[hbm, hbm, vmem, hbm, hbm, hbm],
        out_specs=vmem,
        scratch_shapes=[
            pltpu.VMEM(species.shape, jnp.float32),
            pltpu.VMEM(rate_matrices.shape, jnp.float32),
            pltpu.SMEM(sweeps.shape, jnp.int32),
            pltpu.VMEM(flow_rows.shape, jnp.float32),
            pltpu.VMEM(flow_columns.shape, jnp.float32),
            pltpu.SemaphoreType.DMA((5,)),
            padded,
            padded,
            pltpu.VMEM((nx + 4, ny + 4, 8, depth), jnp.float32),
            pltpu.VMEM((nx * ny * count, 128), jnp.float32),
        ]
        + [pltpu.SemaphoreType.DMA((len(ways),))] * 4,
        compiler_params=pltpu.CompilerParams(
            collective_id=0, has_side_effects=True, vmem_limit_bytes=60 * 2**20
        ),
        name="slab",
    )(species, rate_matrices, loss_rates.reshape(1, count), sweeps, flow_rows, flow_columns)


def solution(mesh):
    placed = (
        P(None, "gx", "gy", None),
        P("gx", "gy", None),
        P(),
        P("gx", "gy"),
        P("gx", "gy", None),
        P("gx", "gy", None),
    )
    extent = (mesh.shape["gx"], mesh.shape["gy"])
    return jax.shard_map(
        functools.partial(on_device, extent), mesh=mesh, in_specs=placed, out_specs=P(None, "gx", "gy", None), check_vma=False
    )
```
